32 devices in a mesh: gx: 16 (over z, x, core), gy: 2 (over y).
Axes of the slice: x: 2, y: 2, z: 4, core: 2. Of those that a mesh axis runs over, the one named last changes fastest.
Arguments:
- velocity: float32 [3, 32, 384, 128], P(None, 'gx', 'gy'), may hold values from -0.8 to 2.3
- stiffness: float32 [2], P('gy'), may hold values from 100 to 100000
- block_inverse: float32 [3, 384, 192], P(None, 'gy'), as said below
Outputs:
- velocity_next: float32 [3, 32, 384, 128], P(None, 'gx', 'gy')
The draws below stay inside these ranges and needn't reach their ends.
Inputs may be any that keep to these rules, and one draw needn't show every extreme that they name: block_inverse[s] for block k is, to float32 rounding, the inverse of the 192-row matrix with 1 + 2 b on its diagonal and -b beside it, b = alpha_s stiffness[k].
All inputs are finite; a program needn't handle non-finite values.
Results may differ from the reference program's by a relative error of at most 0.0003.
Values sent between devices are 32-bit elements; how exact they have to be, the bound alone decides.
A program may use at most 64 MiB of HBM per device.

```python
import math
import jax
import jax.numpy as jnp
from jax import lax

CY = 192
NZ = 128
SUBSTEPS = 3
BLOCKS = 2
NX = 32
NY = 384
N_GY = 2


def stiffness_values(key):
    order = jax.random.permutation(jax.random.fold_in(key, 11), BLOCKS)
    spread = jax.random.uniform(jax.random.fold_in(key, 12), (BLOCKS,), jnp.float32)
    level = (order.astype(jnp.float32) + spread) / BLOCKS
    return 100.0 * jnp.exp(level * math.log(1000.0))


def draw_velocity(key, part):
    rows = (jnp.arange(NY).astype(jnp.float32) + 0.5) / NY
    profile = jnp.sin(math.pi * rows)[None, None, :, None]
    rough = 0.2 * jnp.clip(jax.random.normal(jax.random.fold_in(key, 21), (3, NX, NY, NZ), jnp.float32), -4.0, 4.0)
    levels = jnp.array([1.5, 0.0, 0.0], jnp.float32)
    return levels[:, None, None, None] * profile + rough


def draw_stiffness(key, part):
    return stiffness_values(key)


def draw_block_inverse(key, part):
    values = stiffness_values(key)
    shares = jnp.array([8.0 / 15.0, 2.0 / 15.0, 1.0 / 3.0], jnp.float32)
    strength = (shares[:, None] * values[None, :])[:, :, None, None]
    half_ratio = 0.5 / jnp.sqrt(strength)
    squared = half_ratio * half_ratio
    theta = 2.0 * jnp.log1p(half_ratio + squared / (1.0 + jnp.sqrt(1.0 + squared)))
    rows = jnp.arange(1, CY + 1).astype(jnp.float32)
    smaller = jnp.minimum(rows[:, None], rows[None, :])
    larger = jnp.maximum(rows[:, None], rows[None, :])
    upper_part = jnp.sinh(smaller * theta) * jnp.sinh((CY + 1.0 - larger) * theta)
    lower_part = strength * jnp.sinh(theta) * jnp.sinh((CY + 1.0) * theta)
    table = upper_part / lower_part
    return table.reshape(3, BLOCKS * CY, CY).astype(jnp.float32)


def setup_inputs(seed: int = 0) -> dict:
    key_of = jax.random.split(jax.random.key(seed), 4)
    velocity = draw_velocity(jax.random.fold_in(key_of[3], 71), 0)
    stiffness = draw_stiffness(jax.random.fold_in(key_of[3], 71), 0)
    block_inverse = draw_block_inverse(jax.random.fold_in(key_of[3], 71), 0)
    return {"velocity": velocity, "stiffness": stiffness, "block_inverse": block_inverse}


implicit_share = (8.0 / 15.0, 2.0 / 15.0, 1.0 / 3.0)
new_weight = (8.0 / 15.0, 5.0 / 12.0, 3.0 / 4.0)
old_weight = (0.0, -17.0 / 60.0, -5.0 / 12.0)
courant = (0.3, 0.2, 0.3)


def upwind(field, back_two, back_one, ahead_one, ahead_two, speed):
    behind = 1.5 * field - 2.0 * back_one + 0.5 * back_two
    ahead = -1.5 * field + 2.0 * ahead_one - 0.5 * ahead_two
    return jnp.maximum(speed, 0.0) * behind + jnp.minimum(speed, 0.0) * ahead


def reduced(first_vals, last_vals, tips):
    count = first_vals.shape[0]
    prev_q = jnp.zeros((), jnp.float32)
    prev_last = jnp.zeros_like(first_vals[0])
    fronts, backs, front_qs, back_qs = [], [], [], []
    for block in range(count):
        head_v = tips[0][block]
        tail_v = tips[1][block]
        head_w = tips[2][block]
        tail_w = tips[3][block]
        pivot = 1.0 - head_v * prev_q
        front = (first_vals[block] - head_v * prev_last) / pivot
        back = last_vals[block] - tail_v * prev_last + tail_v * prev_q * front
        front_q = head_w / pivot
        back_q = tail_w + tail_v * prev_q * front_q
        fronts.append(front)
        backs.append(back)
        front_qs.append(front_q)
        back_qs.append(back_q)
        prev_q = back_q
        prev_last = back
    heads = [None] * count
    tails = [None] * count
    heads[count - 1] = fronts[count - 1]
    tails[count - 1] = backs[count - 1]
    for block in range(count - 2, -1, -1):
        after = heads[block + 1]
        heads[block] = fronts[block] - front_qs[block] * after
        tails[block] = backs[block] - back_qs[block] * after
    zero = jnp.zeros_like(first_vals[0])
    lower_prev = jnp.stack([zero] + tails[:-1])
    upper_next = jnp.stack(heads[1:] + [zero])
    return lower_prev, upper_next


def reference(velocity, stiffness, block_inverse):
    count = N_GY
    inverse = block_inverse.reshape(SUBSTEPS, count, CY, CY)
    block_ids = jnp.arange(count)
    first_flag = (block_ids > 0).astype(jnp.float32)
    last_flag = (block_ids < count - 1).astype(jnp.float32)
    row_stiff = jnp.repeat(stiffness, CY)[None, :, None]
    current = velocity
    previous = jnp.zeros_like(velocity)
    for step in range(SUBSTEPS):
        speed_x = current[0]
        speed_y = current[1]
        speed_z = current[2]

        def component(pair):
            field, earlier = pair
            along_x = upwind(field, jnp.roll(field, 2, 0), jnp.roll(field, 1, 0), jnp.roll(field, -1, 0), jnp.roll(field, -2, 0), speed_x)
            padded = jnp.pad(field, ((0, 0), (2, 2), (0, 0)))
            along_y = upwind(field, padded[:, 0:-4], padded[:, 1:-3], padded[:, 3:-1], padded[:, 4:], speed_y)
            along_z = upwind(field, jnp.roll(field, 2, 2), jnp.roll(field, 1, 2), jnp.roll(field, -1, 2), jnp.roll(field, -2, 2), speed_z)
            advect = courant[0] * along_x + courant[1] * along_y + courant[2] * along_z
            diffuse = row_stiff * (padded[:, 3:-1] - 2.0 * field + padded[:, 1:-3])
            forcing = field + implicit_share[step] * diffuse - new_weight[step] * advect - old_weight[step] * earlier
            return forcing, advect

        forcing, previous = lax.map(component, (current, previous))
        shaped = forcing.reshape(3, NX, count, CY, NZ)
        solved = jnp.einsum("kij,cxkjz->cxkiz", inverse[step], shaped, precision=lax.Precision.HIGHEST)
        coupling = -implicit_share[step] * stiffness
        lower = coupling * first_flag
        upper = coupling * last_flag
        column_v = inverse[step][:, :, 0] * lower[:, None]
        column_w = inverse[step][:, :, -1] * upper[:, None]
        tips = (column_v[:, 0], column_v[:, -1], column_w[:, 0], column_w[:, -1])
        first_vals = jnp.moveaxis(solved[:, :, :, 0, :], 2, 0)
        last_vals = jnp.moveaxis(solved[:, :, :, -1, :], 2, 0)
        lower_prev, upper_next = reduced(first_vals, last_vals, tips)
        lower_prev = jnp.moveaxis(lower_prev, 0, 2)[:, :, :, None, :]
        upper_next = jnp.moveaxis(upper_next, 0, 2)[:, :, :, None, :]
        result = solved - column_v[None, None, :, :, None] * lower_prev - column_w[None, None, :, :, None] * upper_next
        current = result.reshape(3, NX, NY, NZ)
    return current
```

```python
import functools

import jax
import jax.numpy as jnp
from jax import lax
from jax.experimental import pallas as pl
from jax.experimental.pallas import tpu as pltpu
from jax.sharding import PartitionSpec as P

SUBSTEPS = 3
PAD = 8
MESH = pl.DeviceIdType.MESH

implicit_share = (8.0 / 15.0, 2.0 / 15.0, 1.0 / 3.0)
new_weight = (8.0 / 15.0, 5.0 / 12.0, 3.0 / 4.0)
old_weight = (0.0, -17.0 / 60.0, -5.0 / 12.0)
courant = (0.3, 0.2, 0.3)


def eliminate(edges, tips, planes, own):
    count = len(edges)
    zero = jnp.zeros_like(edges[0][0:planes])
    row = lambda b, r: edges[b][r * planes : (r + 1) * planes]
    v = lambda b, r: tips[b][r : r + 1]
    w = lambda b, r: tips[b][4 + r : 5 + r]
    prev_q, prev_last = jnp.zeros_like(tips[0][0:1]), zero
    fronts, backs, front_qs, back_qs = [], [], [], []
    for b in range(count):
        pivot = 1.0 - v(b, 0) * prev_q
        front = (row(b, 0) - v(b, 0) * prev_last) / pivot
        back = row(b, 3) - v(b, 3) * prev_last + v(b, 3) * prev_q * front
        front_q = w(b, 0) / pivot
        back_q = w(b, 3) + v(b, 3) * prev_q * front_q
        fronts.append(front)
        backs.append(back)
        front_qs.append(front_q)
        back_qs.append(back_q)
        prev_q, prev_last = back_q, back
    heads, tails = [None] * count, [None] * count
    heads[-1], tails[-1] = fronts[-1], backs[-1]
    for b in range(count - 2, -1, -1):
        heads[b] = fronts[b] - front_qs[b] * heads[b + 1]
        tails[b] = backs[b] - back_qs[b] * heads[b + 1]
    before = [zero] + tails[:-1]
    after = heads[1:] + [zero]

    def solved(b, r):
        return row(b, r) - v(b, r) * before[b] - w(b, r) * after[b]

    def pick(values):
        out = values[0]
        for b in range(1, count):
            out = jnp.where(own == b, values[b], out)
        return out

    above = [pick([zero] + [solved(b, r) for b in range(count - 1)]) for r in (2, 3)]
    below = [pick([solved(b, r) for b in range(1, count)] + [zero]) for r in (0, 1)]
    return pick(before), pick(after), above, below


def kernel(
    n_x,
    n_y,
    stiff_ref,
    vel_ref,
    inv_ref,
    out_ref,
    u_ref,
    left_ref,
    right_ref,
    prev_ref,
    rhs_ref,
    g_ref,
    v_ref,
    w_ref,
    raw_ref,
    edge_ref,
    tip_ref,
    x_send,
    x_recv,
    raw_send,
    raw_recv,
    edge_send,
    edge_recv,
    tip_send,
    tip_recv,
):
    comps, planes, rows, lanes = vel_ref.shape
    me_x, me_y = lax.axis_index("gx"), lax.axis_index("gy")
    right, left = lax.rem(me_x + 1, n_x), lax.rem(me_x + n_x - 1, n_x)
    others = [lax.rem(me_y + off, n_y) for off in range(1, n_y)]
    chunk = 32 if rows % 32 == 0 else 8
    chunks = rows // chunk

    barrier = pltpu.get_barrier_semaphore()
    for side in (left, right):
        pl.semaphore_signal(barrier, inc=1, device_id={"gx": side}, device_id_type=MESH)
    for other in others:
        pl.semaphore_signal(barrier, inc=1, device_id={"gy": other}, device_id_type=MESH)
    pl.semaphore_wait(barrier, 2 + len(others))

    def x_copies(step, c):
        if step == 0:
            tail, head = vel_ref.at[c, planes - 2 : planes], vel_ref.at[c, 0:2]
        else:
            tail = u_ref.at[step, c, planes - 2 : planes, PAD : PAD + rows]
            head = u_ref.at[step, c, 0:2, PAD : PAD + rows]
        return [
            pltpu.make_async_remote_copy(
                tail, left_ref.at[step, c], x_send.at[step, c, 0], x_recv.at[step, c, 0],
                device_id={"gx": right}, device_id_type=MESH,
            ),
            pltpu.make_async_remote_copy(
                head, right_ref.at[step, c], x_send.at[step, c, 1], x_recv.at[step, c, 1],
                device_id={"gx": left}, device_id_type=MESH,
            ),
        ]

    def y_copies(ref, send, recv):
        return [
            pltpu.make_async_remote_copy(
                ref.at[me_y], ref.at[me_y], send.at[i], recv.at[i],
                device_id={"gy": other}, device_id_type=MESH,
            )
            for i, other in enumerate(others)
        ]

    def edge_copies(step, c):
        return y_copies(edge_ref.at[step, c], edge_send.at[step, c], edge_recv.at[step, c])

    for c in range(comps):
        for copy in x_copies(0, c):
            copy.start()
    for c in range(comps):
        for i, at in enumerate((0, 1, rows - 2, rows - 1)):
            for p in range(planes):
                raw_ref[me_y, c, i * planes + p : i * planes + p + 1, :] = vel_ref[c, p, at : at + 1, :]
    raw_copies = y_copies(raw_ref, raw_send, raw_recv)
    for copy in raw_copies:
        copy.start()
    stiff = stiff_ref[0]
    lower_flag = jnp.where(me_y > 0, 1.0, 0.0)
    upper_flag = jnp.where(me_y < n_y - 1, 1.0, 0.0)
    for s in range(SUBSTEPS):
        coupling = -implicit_share[s] * stiff
        column_v = inv_ref[s, :, 0:1] * (coupling * lower_flag)
        column_w = inv_ref[s, :, rows - 1 : rows] * (coupling * upper_flag)
        v_ref[s] = jnp.broadcast_to(column_v, (rows, lanes))
        w_ref[s] = jnp.broadcast_to(column_w, (rows, lanes))
        for i, at in enumerate((0, 1, rows - 2, rows - 1)):
            tip_ref[me_y, s, i : i + 1, :] = v_ref[s, at : at + 1, :]
            tip_ref[me_y, s, 4 + i : 5 + i, :] = w_ref[s, at : at + 1, :]
    tip_copies = y_copies(tip_ref, tip_send, tip_recv)
    for copy in tip_copies:
        copy.start()
    for c in range(comps):
        for p in range(planes):
            u_ref[0, c, p, PAD : PAD + rows, :] = vel_ref[c, p]

    def store_halo(step, c, above, below):
        for p in range(planes):
            for i in range(2):
                u_ref[step, c, p, PAD - 2 + i : PAD - 1 + i, :] = above[i][p : p + 1]
                u_ref[step, c, p, PAD + rows + i : PAD + rows + 1 + i, :] = below[i][p : p + 1]

    for copy in raw_copies:
        copy.wait()
    for c in range(comps):
        zero = jnp.zeros((planes, lanes), jnp.float32)
        above, below = [zero, zero], [zero, zero]
        for b in range(n_y):
            tile = raw_ref[b, c]
            for i in range(2):
                first = tile[i * planes : (i + 1) * planes]
                last = tile[(2 + i) * planes : (3 + i) * planes]
                above[i] = jnp.where(me_y == b + 1, last, above[i])
                below[i] = jnp.where(me_y == b - 1, first, below[i])
        store_halo(0, c, above, below)
    for copy in tip_copies:
        copy.wait()

    def force(step, c):
        copies = x_copies(step, c)
        for copy in copies:
            copy.wait_recv()

        @pl.loop(0, chunks)
        def _(k):
            base = pl.multiple_of(k * chunk, chunk)
            inner = pl.ds(base, chunk)
            own = pl.ds(pl.multiple_of(base + PAD, 8), chunk)
            for p in range(planes):
                def plane(i):
                    if i < 0:
                        return left_ref[step, c, 2 + i, inner, :]
                    if i >= planes:
                        return right_ref[step, c, i - planes, inner, :]
                    return u_ref[step, c, i, own, :]

                speed = [u_ref[step, d, p, own, :] for d in range(comps)]
                weight = [(0.5 * courant[d]) * jnp.abs(speed[d]) for d in range(comps)]
                window = u_ref[step, c, p, pl.ds(base, chunk + 2 * PAD), :]
                at = lambda i: window[PAD + i : PAD + i + chunk]
                field = at(0)
                y1, y_1 = at(1), at(-1)
                turn = lambda i: pltpu.roll(field, i % lanes, 1)
                total = 3.0 * field * (weight[0] + weight[1] + weight[2])
                for d, (m2, m1, p1, p2) in enumerate(
                    (
                        (plane(p - 2), plane(p - 1), plane(p + 1), plane(p + 2)),
                        (at(-2), y_1, y1, at(2)),
                        (turn(2), turn(1), turn(-1), turn(-2)),
                    )
                ):
                    up = speed[d] > 0.0
                    total = total + weight[d] * (
                        jnp.where(up, m2, p2) - 4.0 * jnp.where(up, m1, p1)
                    )
                diffuse = stiff * (y1 - 2.0 * field + y_1)
                forcing = field + implicit_share[step] * diffuse - new_weight[step] * total
                if step > 0:
                    forcing = forcing - old_weight[step] * prev_ref[c, p, inner, :]
                if step < SUBSTEPS - 1:
                    prev_ref[c, p, inner, :] = total
                rhs_ref[c, inner, p * lanes : (p + 1) * lanes] = forcing

        g_ref[c] = jnp.dot(
            inv_ref[step], rhs_ref[c],
            precision=lax.Precision.HIGHEST, preferred_element_type=jnp.float32,
        )
        for i, at in enumerate((0, 1, rows - 2, rows - 1)):
            for p in range(planes):
                edge_ref[step, c, me_y, i * planes + p : i * planes + p + 1, :] = g_ref[
                    c, at : at + 1, p * lanes : (p + 1) * lanes
                ]
        for copy in edge_copies(step, c):
            copy.start()

    def finish(step, c):
        for copy in edge_copies(step, c):
            copy.wait_recv()
        before, after, above, below = eliminate(
            [edge_ref[step, c, b] for b in range(n_y)],
            [tip_ref[b, step] for b in range(n_y)],
            planes,
            me_y,
        )

        @pl.loop(0, chunks)
        def _(k):
            base = pl.multiple_of(k * chunk, chunk)
            inner = pl.ds(base, chunk)
            own = pl.ds(pl.multiple_of(base + PAD, 8), chunk)
            for p in range(planes):
                fresh = (
                    g_ref[c, inner, p * lanes : (p + 1) * lanes]
                    - v_ref[step, inner, :] * before[p : p + 1]
                    - w_ref[step, inner, :] * after[p : p + 1]
                )
                if step < SUBSTEPS - 1:
                    u_ref[step + 1, c, p, own, :] = fresh
                else:
                    out_ref[c, p, inner, :] = fresh

        if step < SUBSTEPS - 1:
            for copy in x_copies(step + 1, c):
                copy.start()
            store_halo(step + 1, c, above, below)

    for step in range(SUBSTEPS):
        for c in range(comps):
            force(step, c)
            if c > 0:
                finish(step, c - 1)
        finish(step, comps - 1)

    for step in range(SUBSTEPS):
        for c in range(comps):
            for copy in x_copies(step, c) + edge_copies(step, c):
                copy.wait_send()


def body(n_x, n_y, velocity, stiffness, block_inverse):
    comps, planes, rows, lanes = velocity.shape
    tile = 4 * planes
    links = n_y - 1
    vmem = lambda *shape: pltpu.VMEM(shape, jnp.float32)
    return pl.pallas_call(
        functools.partial(kernel, n_x, n_y),
        out_shape=jax.ShapeDtypeStruct(velocity.shape, jnp.float32),
        in_specs=[
            pl.BlockSpec(memory_space=pltpu.SMEM),
            pl.BlockSpec(memory_space=pltpu.VMEM),
            pl.BlockSpec(memory_space=pltpu.VMEM),
        ],
        out_specs=pl.BlockSpec(memory_space=pltpu.VMEM),
        scratch_shapes=[
            vmem(SUBSTEPS, comps, planes, rows + 2 * PAD, lanes),
            vmem(SUBSTEPS, comps, 2, rows, lanes),
            vmem(SUBSTEPS, comps, 2, rows, lanes),
            vmem(comps, planes, rows, lanes),
            vmem(comps, rows, planes * lanes),
            vmem(comps, rows, planes * lanes),
            vmem(SUBSTEPS, rows, lanes),
            vmem(SUBSTEPS, rows, lanes),
            vmem(n_y, comps, tile, lanes),
            vmem(SUBSTEPS, comps, n_y, tile, lanes),
            vmem(n_y, SUBSTEPS, 8, lanes),
            pltpu.SemaphoreType.DMA((SUBSTEPS, comps, 2)),
            pltpu.SemaphoreType.DMA((SUBSTEPS, comps, 2)),
            pltpu.SemaphoreType.DMA((links,)),
            pltpu.SemaphoreType.DMA((links,)),
            pltpu.SemaphoreType.DMA((SUBSTEPS, comps, links)),
            pltpu.SemaphoreType.DMA((SUBSTEPS, comps, links)),
            pltpu.SemaphoreType.DMA((links,)),
            pltpu.SemaphoreType.DMA((links,)),
        ],
        compiler_params=pltpu.CompilerParams(
            collective_id=0, has_side_effects=True, vmem_limit_bytes=40 * 1024 * 1024
        ),
    )(stiffness, velocity, block_inverse)


def solution(mesh):
    return jax.shard_map(
        functools.partial(body, mesh.shape["gx"], mesh.shape["gy"]),
        mesh=mesh,
        in_specs=(P(None, "gx", "gy", None), P("gy"), P(None, "gy", None)),
        out_specs=P(None, "gx", "gy", None),
        check_vma=False,
    )
```

```python
import functools

import jax
import jax.numpy as jnp
from jax import lax
from jax.experimental import pallas as pl
from jax.experimental.pallas import tpu as pltpu
from jax.sharding import PartitionSpec as P

SUBSTEPS = 3
PAD = 8
MESH = pl.DeviceIdType.MESH

implicit_share = (8.0 / 15.0, 2.0 / 15.0, 1.0 / 3.0)
new_weight = (8.0 / 15.0, 5.0 / 12.0, 3.0 / 4.0)
old_weight = (0.0, -17.0 / 60.0, -5.0 / 12.0)
courant = (0.3, 0.2, 0.3)


def eliminate(edges, tips, planes, own):
    count = len(edges)
    zero = jnp.zeros_like(edges[0][0:planes])
    row = lambda b, r: edges[b][r * planes : (r + 1) * planes]
    v = lambda b, r: tips[b][r : r + 1]
    w = lambda b, r: tips[b][4 + r : 5 + r]
    prev_q, prev_last = jnp.zeros_like(tips[0][0:1]), zero
    fronts, backs, front_qs, back_qs = [], [], [], []
    for b in range(count):
        pivot = 1.0 - v(b, 0) * prev_q
        front = (row(b, 0) - v(b, 0) * prev_last) / pivot
        back = row(b, 3) - v(b, 3) * prev_last + v(b, 3) * prev_q * front
        front_q = w(b, 0) / pivot
        back_q = w(b, 3) + v(b, 3) * prev_q * front_q
        fronts.append(front)
        backs.append(back)
        front_qs.append(front_q)
        back_qs.append(back_q)
        prev_q, prev_last = back_q, back
    heads, tails = [None] * count, [None] * count
    heads[-1], tails[-1] = fronts[-1], backs[-1]
    for b in range(count - 2, -1, -1):
        heads[b] = fronts[b] - front_qs[b] * heads[b + 1]
        tails[b] = backs[b] - back_qs[b] * heads[b + 1]
    before = [zero] + tails[:-1]
    after = heads[1:] + [zero]

    def solved(b, r):
        return row(b, r) - v(b, r) * before[b] - w(b, r) * after[b]

    def pick(values):
        out = values[0]
        for b in range(1, count):
            out = jnp.where(own == b, values[b], out)
        return out

    above = [pick([zero] + [solved(b, r) for b in range(count - 1)]) for r in (2, 3)]
    below = [pick([solved(b, r) for b in range(1, count)] + [zero]) for r in (0, 1)]
    return pick(before), pick(after), above, below


def kernel(
    n_x,
    n_y,
    stiff_ref,
    vel_ref,
    inv_hbm,
    out_ref,
    inv_ref,
    u_ref,
    left_ref,
    right_ref,
    prev_ref,
    rhs_ref,
    g_ref,
    v_ref,
    w_ref,
    raw_ref,
    edge_ref,
    tip_ref,
    x_send,
    x_recv,
    raw_send,
    raw_recv,
    edge_send,
    edge_recv,
    tip_send,
    tip_recv,
    local_sem,
):
    comps, planes, rows, lanes = vel_ref.shape
    me_x, me_y = lax.axis_index("gx"), lax.axis_index("gy")
    right, left = lax.rem(me_x + 1, n_x), lax.rem(me_x + n_x - 1, n_x)
    others = [lax.rem(me_y + off, n_y) for off in range(1, n_y)]
    chunk = next(size for size in (64, 32, 16, 8) if rows % size == 0)
    chunks = rows // chunk

    own_copy = pltpu.make_async_copy(
        vel_ref, u_ref.at[0, :, :, PAD : PAD + rows], local_sem.at[0]
    )
    inv_copy = pltpu.make_async_copy(inv_hbm, inv_ref, local_sem.at[1])
    own_copy.start()
    inv_copy.start()
    barrier = pltpu.get_barrier_semaphore()
    for side in (left, right):
        pl.semaphore_signal(barrier, inc=1, device_id={"gx": side}, device_id_type=MESH)
    for other in others:
        pl.semaphore_signal(barrier, inc=1, device_id={"gy": other}, device_id_type=MESH)
    pl.semaphore_wait(barrier, 2 + len(others))

    def x_copies(step, c):
        if step == 0:
            tail, head = vel_ref.at[c, planes - 2 : planes], vel_ref.at[c, 0:2]
        else:
            tail = u_ref.at[step, c, planes - 2 : planes, PAD : PAD + rows]
            head = u_ref.at[step, c, 0:2, PAD : PAD + rows]
        return [
            pltpu.make_async_remote_copy(
                tail, left_ref.at[step, c], x_send.at[step, c, 0], x_recv.at[step, c, 0],
                device_id={"gx": right}, device_id_type=MESH,
            ),
            pltpu.make_async_remote_copy(
                head, right_ref.at[step, c], x_send.at[step, c, 1], x_recv.at[step, c, 1],
                device_id={"gx": left}, device_id_type=MESH,
            ),
        ]

    def y_copies(ref, send, recv):
        return [
            pltpu.make_async_remote_copy(
                ref.at[me_y], ref.at[me_y], send.at[i], recv.at[i],
                device_id={"gy": other}, device_id_type=MESH,
            )
            for i, other in enumerate(others)
        ]

    def edge_copies(step, c):
        return y_copies(edge_ref.at[step, c], edge_send.at[step, c], edge_recv.at[step, c])

    for c in range(comps):
        for copy in x_copies(0, c):
            copy.start()
    own_copy.wait()
    for c in range(comps):
        for i, at in enumerate((0, 1, rows - 2, rows - 1)):
            for p in range(planes):
                raw_ref[me_y, c, i * planes + p : i * planes + p + 1, :] = u_ref[
                    0, c, p, PAD + at : PAD + at + 1, :
                ]
    raw_copies = y_copies(raw_ref, raw_send, raw_recv)
    for copy in raw_copies:
        copy.start()
    inv_copy.wait()
    stiff = stiff_ref[0]
    lower_flag = jnp.where(me_y > 0, 1.0, 0.0)
    upper_flag = jnp.where(me_y < n_y - 1, 1.0, 0.0)
    for s in range(SUBSTEPS):
        coupling = -implicit_share[s] * stiff
        column_v = inv_ref[s, :, 0:1] * (coupling * lower_flag)
        column_w = inv_ref[s, :, rows - 1 : rows] * (coupling * upper_flag)
        v_ref[s] = jnp.broadcast_to(column_v, (rows, lanes))
        w_ref[s] = jnp.broadcast_to(column_w, (rows, lanes))
        for i, at in enumerate((0, 1, rows - 2, rows - 1)):
            tip_ref[me_y, s, i : i + 1, :] = v_ref[s, at : at + 1, :]
            tip_ref[me_y, s, 4 + i : 5 + i, :] = w_ref[s, at : at + 1, :]
    tip_copies = y_copies(tip_ref, tip_send, tip_recv)
    for copy in tip_copies:
        copy.start()

    def store_halo(step, c, above, below):
        for p in range(planes):
            for i in range(2):
                u_ref[step, c, p, PAD - 2 + i : PAD - 1 + i, :] = above[i][p : p + 1]
                u_ref[step, c, p, PAD + rows + i : PAD + rows + 1 + i, :] = below[i][p : p + 1]

    for copy in raw_copies:
        copy.wait()
    for c in range(comps):
        zero = jnp.zeros((planes, lanes), jnp.float32)
        above, below = [zero, zero], [zero, zero]
        for b in range(n_y):
            tile = raw_ref[b, c]
            for i in range(2):
                first = tile[i * planes : (i + 1) * planes]
                last = tile[(2 + i) * planes : (3 + i) * planes]
                above[i] = jnp.where(me_y == b + 1, last, above[i])
                below[i] = jnp.where(me_y == b - 1, first, below[i])
        store_halo(0, c, above, below)
    for copy in tip_copies:
        copy.wait()

    def prepare(step, c):
        @pl.loop(0, chunks)
        def _(k):
            base = pl.multiple_of(k * chunk, chunk)
            inner = pl.ds(base, chunk)
            own = pl.ds(pl.multiple_of(base + PAD, 8), chunk)
            for p in range(planes):
                speed = [u_ref[step, d, p, own, :] for d in range(comps)]
                weight = [(0.5 * courant[d]) * jnp.abs(speed[d]) for d in range(comps)]
                window = u_ref[step, c, p, pl.ds(base, chunk + 2 * PAD), :]
                at = lambda i: window[PAD + i : PAD + i + chunk]
                field = at(0)
                y1, y_1 = at(1), at(-1)
                turn = lambda i: pltpu.roll(field, i % lanes, 1)
                total = 3.0 * field * (weight[0] + weight[1] + weight[2])
                for d, (m2, m1, p1, p2) in (
                    (1, (at(-2), y_1, y1, at(2))),
                    (2, (turn(2), turn(1), turn(-1), turn(-2))),
                ):
                    up = speed[d] > 0.0
                    total = total + weight[d] * (
                        jnp.where(up, m2, p2) - 4.0 * jnp.where(up, m1, p1)
                    )
                diffuse = stiff * (y1 - 2.0 * field + y_1)
                forcing = field + implicit_share[step] * diffuse - new_weight[step] * total
                if step > 0:
                    forcing = forcing - old_weight[step] * prev_ref[c, p, inner, :]
                if step < SUBSTEPS - 1:
                    prev_ref[c, p, inner, :] = total
                rhs_ref[c, inner, p * lanes : (p + 1) * lanes] = forcing

    def force(step, c):
        for copy in x_copies(step, c):
            copy.wait_recv()

        @pl.loop(0, chunks)
        def _(k):
            base = pl.multiple_of(k * chunk, chunk)
            inner = pl.ds(base, chunk)
            own = pl.ds(pl.multiple_of(base + PAD, 8), chunk)
            for p in range(planes):

                def plane(i):
                    if i < 0:
                        return left_ref[step, c, 2 + i, inner, :]
                    if i >= planes:
                        return right_ref[step, c, i - planes, inner, :]
                    return u_ref[step, c, i, own, :]

                speed = u_ref[step, 0, p, own, :]
                up = speed > 0.0
                along = (0.5 * courant[0]) * jnp.abs(speed) * (
                    jnp.where(up, plane(p - 2), plane(p + 2))
                    - 4.0 * jnp.where(up, plane(p - 1), plane(p + 1))
                )
                if step < SUBSTEPS - 1:
                    prev_ref[c, p, inner, :] += along
                rhs_ref[c, inner, p * lanes : (p + 1) * lanes] -= new_weight[step] * along

        g_ref[c] = jnp.dot(
            inv_ref[step], rhs_ref[c],
            precision=lax.Precision.HIGHEST, preferred_element_type=jnp.float32,
        )
        for i, at in enumerate((0, 1, rows - 2, rows - 1)):
            for p in range(planes):
                edge_ref[step, c, me_y, i * planes + p : i * planes + p + 1, :] = g_ref[
                    c, at : at + 1, p * lanes : (p + 1) * lanes
                ]
        for copy in edge_copies(step, c):
            copy.start()

    def finish(step, c):
        for copy in edge_copies(step, c):
            copy.wait_recv()
        before, after, above, below = eliminate(
            [edge_ref[step, c, b] for b in range(n_y)],
            [tip_ref[b, step] for b in range(n_y)],
            planes,
            me_y,
        )

        @pl.loop(0, chunks)
        def _(k):
            base = pl.multiple_of(k * chunk, chunk)
            inner = pl.ds(base, chunk)
            own = pl.ds(pl.multiple_of(base + PAD, 8), chunk)
            for p in range(planes):
                fresh = (
                    g_ref[c, inner, p * lanes : (p + 1) * lanes]
                    - v_ref[step, inner, :] * before[p : p + 1]
                    - w_ref[step, inner, :] * after[p : p + 1]
                )
                if step < SUBSTEPS - 1:
                    u_ref[step + 1, c, p, own, :] = fresh
                else:
                    out_ref[c, p, inner, :] = fresh

        if step < SUBSTEPS - 1:
            for copy in x_copies(step + 1, c):
                copy.start()
            store_halo(step + 1, c, above, below)

    for step in range(SUBSTEPS):
        for c in range(comps):
            prepare(step, c)
            force(step, c)
            if c > 0:
                finish(step, c - 1)
        finish(step, comps - 1)

    for step in range(SUBSTEPS):
        for c in range(comps):
            for copy in x_copies(step, c) + edge_copies(step, c):
                copy.wait_send()


def body(n_x, n_y, velocity, stiffness, block_inverse):
    comps, planes, rows, lanes = velocity.shape
    tile = 4 * planes
    links = n_y - 1
    vmem = lambda *shape: pltpu.VMEM(shape, jnp.float32)
    return pl.pallas_call(
        functools.partial(kernel, n_x, n_y),
        out_shape=jax.ShapeDtypeStruct(velocity.shape, jnp.float32),
        in_specs=[
            pl.BlockSpec(memory_space=pltpu.SMEM),
            pl.BlockSpec(memory_space=pltpu.HBM),
            pl.BlockSpec(memory_space=pltpu.HBM),
        ],
        out_specs=pl.BlockSpec(memory_space=pltpu.VMEM),
        scratch_shapes=[
            vmem(*block_inverse.shape),
            vmem(SUBSTEPS, comps, planes, rows + 2 * PAD, lanes),
            vmem(SUBSTEPS, comps, 2, rows, lanes),
            vmem(SUBSTEPS, comps, 2, rows, lanes),
            vmem(comps, planes, rows, lanes),
            vmem(comps, rows, planes * lanes),
            vmem(comps, rows, planes * lanes),
            vmem(SUBSTEPS, rows, lanes),
            vmem(SUBSTEPS, rows, lanes),
            vmem(n_y, comps, tile, lanes),
            vmem(SUBSTEPS, comps, n_y, tile, lanes),
            vmem(n_y, SUBSTEPS, 8, lanes),
            pltpu.SemaphoreType.DMA((SUBSTEPS, comps, 2)),
            pltpu.SemaphoreType.DMA((SUBSTEPS, comps, 2)),
            pltpu.SemaphoreType.DMA((links,)),
            pltpu.SemaphoreType.DMA((links,)),
            pltpu.SemaphoreType.DMA((SUBSTEPS, comps, links)),
            pltpu.SemaphoreType.DMA((SUBSTEPS, comps, links)),
            pltpu.SemaphoreType.DMA((links,)),
            pltpu.SemaphoreType.DMA((links,)),
            pltpu.SemaphoreType.DMA((2,)),
        ],
        compiler_params=pltpu.CompilerParams(
            collective_id=0, has_side_effects=True, vmem_limit_bytes=62 * 1024 * 1024
        ),
    )(stiffness, velocity, block_inverse)


def solution(mesh):
    return jax.shard_map(
        functools.partial(body, mesh.shape["gx"], mesh.shape["gy"]),
        mesh=mesh,
        in_specs=(P(None, "gx", "gy", None), P("gy"), P(None, "gy", None)),
        out_specs=P(None, "gx", "gy", None),
        check_vma=False,
    )
```
